512 devices in a mesh: px: 32 (over z, y_hi), py: 16 (over x, y_lo, core).
Axes of the slice: x: 4, y: 4 (y_hi: 2, y_lo: 2; y = y_hi * 2 + y_lo), z: 16, core: 2. Of those that a mesh axis runs over, the one named last changes fastest.
Arguments:
- residual: float32 [512, 1792, 128], P('px', 'py'), may hold values from -6 to 6
- basis: float32 [4, 512, 1792], P(None, 'px', 'py'), may hold values from -0.6 to 0.6
- inv_blocks: bfloat16 [32, 16, 32, 3, 128, 128], P('px', 'py'), may hold values from -0.3125 to 0.3125
- pattern: int32 [32, 16, 32, 3], P('px', 'py'), may hold values from 0 to 31
- coarse_map: int32 [32, 16, 4], replicated, may hold values from 0 to 2047
- coarse_inv: float32 [2048, 2048], P(('px', 'py')), may hold values from -0.125 to 0.125
Outputs:
- preconditioned: float32 [512, 1792, 128], P('px', 'py')
The draws below stay inside these ranges and needn't reach their ends.
All inputs are finite; a program needn't handle non-finite values.
Results may differ from the reference program's by a relative error of at most 0.0022.
Values may be sent and summed in bfloat16 or wider, within the bound.
No kernel may reach another device: no remote copies, remote signals or barrier semaphores. Data moves between devices by JAX's collectives and lax.ppermute only.
A program may use at most 64 MiB of HBM per device.

```python
import jax
import jax.numpy as jnp
from jax import lax

CX = 16
CY = 112
W = 8
R = 128
K = 3
NCL = 4
RB = 32
EY = 128
NX = 512
NY = 1792
NC = 2048
N_PX = 32
N_PY = 16


def with_ends(drawn, stream_key, smallest, high):
    spot = [jax.random.randint(jax.random.fold_in(stream_key, axis), (), 0, length) for axis, length in enumerate(drawn.shape)]
    widest = drawn.shape.index(max(drawn.shape))
    next_to = spot[:widest] + [(spot[widest] + 1) % drawn.shape[widest]] + spot[widest + 1:]
    return drawn.at[tuple(spot)].set(smallest).at[tuple(next_to)].set(high)


def level_of(stream_key, dims, shards, smallest, top_value):
    gain = 1.0
    for position, parts in shards:
        heights = jax.random.uniform(jax.random.fold_in(jax.random.fold_in(stream_key, 6), position), (parts,), jnp.float32, smallest / len(shards), top_value / len(shards))
        gain = gain * jnp.repeat(jnp.exp(heights), dims[position] // parts).reshape((-1,) + (1,) * (len(dims) - 1 - position))
    return gain


def bell_draw(key, dims, width, limit, cuts=(), held_as=jnp.bfloat16):
    level = level_of(key, dims, cuts, -0.22, 0.18) if cuts else 1.0
    array = jax.random.normal(key, dims, jnp.float32) * width * level
    return jnp.minimum(jnp.maximum(array, -limit), limit).astype(held_as)


def setup_inputs(seed: int = 0) -> dict:
    arg_keys = jax.random.split(jax.random.key(seed), 7)
    residual = bell_draw(arg_keys[0], (NX, NY, R), 1.0, 6.0, ((0, 32), (1, 16)), jnp.float32)
    basis = bell_draw(arg_keys[1], (NCL, NX, NY), 0.1, 0.6, ((1, 32), (2, 16)), jnp.float32)
    inv_blocks = bell_draw(arg_keys[2], (N_PX, N_PY, RB, K, EY, EY), (K * EY) ** -0.5, 0.3125, ((0, 32), (1, 16)))
    pattern = with_ends(jax.random.randint(arg_keys[3], (N_PX, N_PY, RB, K), 0, RB), jax.random.fold_in(arg_keys[3], 1), 0, RB - 1).astype(jnp.int32)
    coarse_map = with_ends(jax.random.randint(arg_keys[4], (N_PX, N_PY, NCL), 0, NC), jax.random.fold_in(arg_keys[4], 1), 0, NC - 1).astype(jnp.int32)
    coarse_inv = bell_draw(arg_keys[5], (NC, NC), NC ** -0.5, 0.125, ((0, 512),), jnp.float32)
    return dict(residual=residual, basis=basis, inv_blocks=inv_blocks, pattern=pattern, coarse_map=coarse_map, coarse_inv=coarse_inv)


def reference(residual, basis, inv_blocks, pattern, coarse_map, coarse_inv):
    rounded = residual.astype(jnp.bfloat16)
    padded = jnp.pad(rounded, ((W, W), (W, W), (0, 0)))

    def local_block(index):
        row = index // N_PY
        col = index % N_PY
        ext = lax.dynamic_slice(padded, (row * CX, col * CY, jnp.int32(0)), (RB, EY, R))
        picked = jnp.take(ext, pattern[row, col].reshape(-1), axis=0).reshape(RB, K, EY, R)
        solved = jnp.einsum('ikyz,ikzr->iyr', inv_blocks[row, col].astype(jnp.float32), picked.astype(jnp.float32))
        return solved[W:W + CX, W:W + CY]

    blocks = lax.map(local_block, jnp.arange(N_PX * N_PY, dtype=jnp.int32))
    local_part = blocks.reshape(N_PX, N_PY, CX, CY, R).transpose(0, 2, 1, 3, 4).reshape(NX, NY, R)
    shaped_basis = basis.reshape(NCL, N_PX, CX, N_PY, CY)
    shaped_res = residual.reshape(N_PX, CX, N_PY, CY, R)
    contrib = jnp.einsum('lacbd,acbdr->ablr', shaped_basis, shaped_res, precision=lax.Precision.HIGHEST)
    coarse_res = jax.ops.segment_sum(contrib.reshape(-1, R), coarse_map.reshape(-1), num_segments=NC)
    coarse_sol = jnp.dot(coarse_inv, coarse_res, precision=lax.Precision.HIGHEST)
    picked_sol = jnp.take(coarse_sol, coarse_map.reshape(-1), axis=0).reshape(N_PX, N_PY, NCL, R)
    correction = jnp.einsum('lacbd,ablr->acbdr', shaped_basis, picked_sol, precision=lax.Precision.HIGHEST)
    return local_part + correction.reshape(NX, NY, R)
```

```python
import jax
import jax.numpy as jnp
from jax import lax
from jax.sharding import Mesh, PartitionSpec as P

W = 8
K = 3
BF = jnp.bfloat16
F32 = jnp.float32
HIGH = lax.Precision.HIGHEST


def shifted(cells, axis, dim, width):
    count = lax.axis_size(axis)
    ends = count - 1
    head = lax.slice_in_dim(cells, 0, width, axis=dim)
    tail = lax.slice_in_dim(cells, cells.shape[dim] - width, cells.shape[dim], axis=dim)
    return [
        lax.ppermute(tail, axis, [(i, i + 1) for i in range(ends)]),
        cells,
        lax.ppermute(head, axis, [(i + 1, i) for i in range(ends)]),
    ]


def local_solve(rounded, inv_blocks, pattern):
    own_x, own_y, vectors = rounded.shape
    ext = jnp.concatenate(shifted(rounded, "py", 1, W), axis=1)
    ext = jnp.concatenate(shifted(ext, ("z", "h"), 0, W), axis=0)
    wanted = pattern[0, 0, W : W + own_x]
    picked = jnp.take(ext, wanted.reshape(-1), axis=0).reshape(own_x, K, ext.shape[1], vectors)
    solved = jnp.einsum(
        "ikyz,ikzr->iyr", inv_blocks[0, 0, W : W + own_x], picked, preferred_element_type=F32
    )
    return solved[:, W : W + own_y]


def body(residual, basis, inv_blocks, pattern, coarse_map, coarse_inv):
    nz = lax.axis_size("z")
    nh = lax.axis_size("h")
    ny = lax.axis_size("py")
    plane = nh * ny
    ncl, own_x, own_y = basis.shape
    vectors = residual.shape[2]
    total = coarse_inv.shape[1]
    rounded = residual.astype(BF)
    local_part = local_solve(rounded, inv_blocks, pattern)

    ids = coarse_map.reshape(-1)
    spread = (jnp.arange(total, dtype=jnp.int32)[:, None] == ids[None, :]).astype(BF)
    ordered = jnp.dot(coarse_inv.astype(BF), spread, preferred_element_type=F32).astype(BF)
    columns = ordered.reshape(ncl, nz, plane * ncl).transpose(1, 0, 2)
    column = lax.all_to_all(columns, "z", 0, 0)

    me = lax.axis_index("h") * ny + lax.axis_index("py")
    wanted = coarse_map.reshape(nz, plane, ncl).transpose(1, 0, 2).reshape(-1)
    owner = wanted // ncl
    place = jnp.where(owner % plane == me, (owner // plane) * ncl + wanted % ncl, -1)
    pick = (place[:, None] == jnp.arange(nz * ncl)[None, :]).astype(BF)
    sent = jnp.dot(pick, column.reshape(nz * ncl, plane * ncl), preferred_element_type=F32).astype(BF)
    contrib = jnp.einsum("lxy,xyr->lr", basis, residual, precision=HIGH).astype(BF)
    sent = jnp.concatenate(
        [sent.reshape(plane, nz * ncl, plane * ncl), jnp.broadcast_to(contrib, (plane,) + contrib.shape)], axis=1
    )
    got = lax.all_to_all(sent, ("h", "py"), 0, 0)
    needed = jnp.sum(got[:, : nz * ncl].astype(F32), axis=0).astype(BF)
    every = got[:, nz * ncl :].reshape(plane * ncl, vectors)
    partial = jnp.dot(needed, every, preferred_element_type=F32)
    shares = lax.all_to_all(partial.reshape(nz, ncl, vectors), "z", 0, 0)
    local_sol = jnp.sum(shares, axis=0)
    correction = jnp.einsum("lxy,lr->xyr", basis, local_sol, precision=HIGH)
    return local_part + correction


def solution(mesh):
    count_x, count_y = mesh.devices.shape
    fine = Mesh(mesh.devices.reshape(count_x // 2, 2, count_y), ("z", "h", "py"))
    px = ("z", "h")
    return jax.shard_map(
        body,
        mesh=fine,
        in_specs=(
            P(px, "py", None),
            P(None, px, "py"),
            P(px, "py", None, None, None, None),
            P(px, "py", None, None),
            P(),
            P(("z", "h", "py"), None),
        ),
        out_specs=P(px, "py", None),
        check_vma=False,
    )
```

```python
import functools

import jax
import jax.numpy as jnp
from jax import lax
from jax.experimental import pallas as pl
from jax.experimental.pallas import tpu as pltpu
from jax.sharding import Mesh, PartitionSpec as P

W = 8
K = 3
NCL = 4
BF = jnp.bfloat16
F32 = jnp.float32
HIGH = lax.Precision.HIGHEST
VMEM = pl.BlockSpec(memory_space=pltpu.VMEM)
ANYWHERE = pl.BlockSpec(memory_space=pl.ANY)
LARGE = pltpu.CompilerParams(vmem_limit_bytes=60 * 1024 * 1024)
SLOW = pl.CostEstimate(flops=20_000_000_000, bytes_accessed=1_000_000, transcendentals=0)
GRANT = pltpu.CompilerParams(vmem_limit_bytes=32 * 1024 * 1024)


def order_kernel(rows_hbm, map_hbm, out_ref, rows_ref, map_ref, sems):
    fetch_map = pltpu.make_async_copy(map_hbm, map_ref, sems.at[0])
    fetch_rows = pltpu.make_async_copy(rows_hbm, rows_ref, sems.at[1])
    fetch_map.start()
    fetch_rows.start()
    ncl, total = rows_ref.shape
    ny, _, nx = map_ref.shape
    lanes = ncl * nx
    half = lanes // 2
    chunks = total // lanes
    fetch_map.wait()
    flat = jnp.concatenate([map_ref[:, m, :] for m in range(ncl)], axis=1)
    to = lax.broadcasted_iota(jnp.int32, (lanes, lanes), 1)
    h, zm = to // half, to % half
    source = (zm % ncl) * nx + (zm // ncl) * 2 + h
    swap = (lax.broadcasted_iota(jnp.int32, (lanes, lanes), 0) == source).astype(F32).astype(BF)
    upper_bits = (flat // 16).astype(F32).astype(BF)
    lower_bits = (flat % 16).astype(F32).astype(BF)
    ids = jnp.dot(upper_bits, swap, preferred_element_type=F32) * 16.0
    ids = (ids + jnp.dot(lower_bits, swap, preferred_element_type=F32)).astype(jnp.int32)
    fetch_rows.wait()
    upper = lax.broadcasted_iota(jnp.int32, (2 * ncl, lanes), 0) < ncl
    twice = [
        jnp.concatenate([rows_ref[:, s * lanes : (s + 1) * lanes]] * 2, axis=0) for s in range(chunks)
    ]
    done = []
    for pair in range(ny // 2):
        one, two = (jnp.broadcast_to(ids[2 * pair + i : 2 * pair + i + 1, :], upper.shape) for i in (0, 1))
        spot = jnp.where(upper, one, two)
        lane = spot % lanes
        chunk = spot // lanes
        picked = jnp.zeros(upper.shape, F32)
        for s in range(chunks):
            moved = jnp.take_along_axis(twice[s], lane, axis=1, mode="promise_in_bounds")
            picked = jnp.where(chunk == s, moved, picked)
        done.append(picked)
    picked = jnp.concatenate(done, axis=0)
    both = jnp.concatenate([picked, pltpu.roll(picked, half, 1)], axis=0)
    out_ref[...] = both.astype(BF)


def order_columns(rows, by_y):
    ny, ncl, nx = by_y.shape
    return pl.pallas_call(
        order_kernel,
        out_shape=jax.ShapeDtypeStruct((2 * ny * ncl, nx * ncl), BF),
        in_specs=[ANYWHERE, ANYWHERE],
        out_specs=VMEM,
        scratch_shapes=[
            pltpu.VMEM(rows.shape, F32),
            pltpu.VMEM(by_y.shape, jnp.int32),
            pltpu.SemaphoreType.DMA((2,)),
        ],
        compiler_params=LARGE,
    )(rows, by_y)


def route_kernel(held_ref, place_ref, contrib_ref, out_ref):
    held = held_ref.shape[0]
    slots = place_ref.shape[1]
    ncl = contrib_ref.shape[0]
    depth = out_ref.shape[1] - 2 * ncl
    turned = held_ref[...].astype(F32).T[:depth].astype(BF)
    rows = lax.broadcasted_iota(jnp.int32, (held, slots), 0)
    contrib = contrib_ref[...]
    coarse = contrib.astype(BF).astype(F32)
    both = jnp.concatenate([coarse, contrib - coarse], axis=0).astype(BF)
    for z in range(place_ref.shape[0]):
        pick = (rows == place_ref[z : z + 1, :]).astype(F32).astype(BF)
        sent = jnp.dot(turned, pick, preferred_element_type=F32)
        out_ref[z, 0:depth, :] = sent.astype(BF)
        out_ref[z, depth : depth + 2 * ncl, :] = both


def route(held, place, contrib):
    nz, slots = place.shape
    return pl.pallas_call(
        route_kernel,
        out_shape=jax.ShapeDtypeStruct((nz, (nz + 2) * contrib.shape[0], slots), BF),
        in_specs=[VMEM, VMEM, VMEM],
        out_specs=VMEM,
        compiler_params=GRANT,
        cost_estimate=SLOW,
    )(held, place, contrib)


def apply_kernel(got_ref, out_ref):
    nz, rows, lanes = got_ref.shape
    ncl = NCL
    depth = rows - 2 * ncl
    block = got_ref[0, 0:depth, :].astype(F32)
    for z in range(1, nz):
        block += got_ref[z, 0:depth, :].astype(F32)
    upper = lax.broadcasted_iota(jnp.int32, (2 * ncl, lanes), 0) < ncl
    high, low = [], []
    for q in range(nz // 2):
        one = got_ref[2 * q, depth:rows, :].astype(F32)
        two = got_ref[2 * q + 1, depth:rows, :].astype(F32)
        high.append(jnp.where(upper, one, pltpu.roll(two, ncl, 0)))
        low.append(jnp.where(upper, pltpu.roll(one, ncl, 0), two))
    turned = block.T.astype(BF)
    cells = jnp.concatenate(high + low, axis=0).astype(BF)
    out_ref[...] = jnp.dot(
        jnp.concatenate([turned, turned], axis=1), cells, preferred_element_type=F32
    )


def apply_block(got):
    slots = got.shape[2]
    return pl.pallas_call(
        apply_kernel,
        out_shape=jax.ShapeDtypeStruct((slots, slots), F32),
        in_specs=[VMEM],
        out_specs=VMEM,
        compiler_params=GRANT,
        cost_estimate=SLOW,
    )(got)


def round_kernel(cells_ref, after_ref, out_ref):
    out_ref[...] = cells_ref[...].astype(BF)


def round_cells(cells, after):
    block = pl.BlockSpec((cells.shape[0] // 4,) + cells.shape[1:], lambda i: (i, 0, 0))
    return pl.pallas_call(
        round_kernel,
        grid=(4,),
        out_shape=jax.ShapeDtypeStruct(cells.shape, BF),
        in_specs=[block, ANYWHERE],
        out_specs=block,
        compiler_params=GRANT,
    )(cells, after)


def widen_kernel(below_ref, mid_ref, above_ref, first_ref, last_ref):
    rows = first_ref.shape[0]
    for start, out_ref in ((0, first_ref), (rows, last_ref)):
        part = slice(start, start + rows)
        out_ref[...] = jnp.concatenate([below_ref[part], mid_ref[part], above_ref[part]], axis=1)


def widen(below, mid, above):
    wide = below.shape[1] + mid.shape[1] + above.shape[1]
    shape = jax.ShapeDtypeStruct((mid.shape[0] // 2, wide, mid.shape[2]), BF)
    return pl.pallas_call(
        widen_kernel,
        out_shape=(shape, shape),
        in_specs=[VMEM, VMEM, VMEM],
        out_specs=(VMEM, VMEM),
        compiler_params=GRANT,
    )(below, mid, above)


def solve_kernel(pattern_ref, left_ref, first_ref, last_ref, right_ref, inv_ref, after_ref, out_ref, ext_ref):
    step = pl.program_id(0)
    each = out_ref.shape[0]
    own_y = out_ref.shape[1]
    rows = left_ref.shape[0]

    @pl.when(step == 0)
    def _():
        for i, ref in enumerate((left_ref, first_ref, last_ref, right_ref)):
            ext_ref[i * rows : (i + 1) * rows] = ref[...]

    for i in range(each):
        spot = (W + step * each + i) * K
        blocks = jnp.concatenate([inv_ref[0, 0, i, k] for k in range(K)], axis=1)
        cells = jnp.concatenate([ext_ref[pattern_ref[spot + k]] for k in range(K)], axis=0)
        solved = jnp.dot(blocks, cells, preferred_element_type=F32)
        out_ref[i] = solved[W : W + own_y]


def solve(pattern, left, first, last, right, inv_blocks, after, own_y):
    steps = 4
    own_x = 2 * first.shape[0]
    each = own_x // steps
    wide, vectors = first.shape[1:]
    return pl.pallas_call(
        solve_kernel,
        grid_spec=pltpu.PrefetchScalarGridSpec(
            num_scalar_prefetch=1,
            grid=(steps,),
            in_specs=[
                VMEM,
                VMEM,
                VMEM,
                VMEM,
                pl.BlockSpec((1, 1, each, K, wide, wide), lambda i, p: (0, 0, i + W // each, 0, 0, 0)),
                ANYWHERE,
            ],
            out_specs=pl.BlockSpec((each, own_y, vectors), lambda i, p: (i, 0, 0)),
            scratch_shapes=[pltpu.VMEM((2 * own_x, wide, vectors), BF)],
        ),
        out_shape=jax.ShapeDtypeStruct((own_x, own_y, vectors), F32),
        compiler_params=GRANT,
    )(pattern, left, first, last, right, inv_blocks, after)


def finish_kernel(shares_ref, basis_ref, local_ref, out_ref):
    nz, ncl, lanes = shares_ref.shape
    each = out_ref.shape[0]
    start = pl.program_id(0) * each
    sol = shares_ref[0]
    for z in range(1, nz):
        sol += shares_ref[z]
    high = sol.astype(BF).astype(F32)
    terms = jnp.concatenate([high, sol - high, high, jnp.zeros((lanes - 3 * ncl, lanes), F32)], axis=0)
    terms = terms.astype(BF)
    for x in range(each):
        out_ref[x] = local_ref[start + x] + jnp.dot(basis_ref[start + x], terms, preferred_element_type=F32)


def finish(shares, basis, local):
    return pl.pallas_call(
        finish_kernel,
        grid=(4,),
        out_shape=jax.ShapeDtypeStruct(local.shape, F32),
        in_specs=[VMEM, VMEM, VMEM],
        out_specs=pl.BlockSpec((local.shape[0] // 4,) + local.shape[1:], lambda i: (i, 0, 0)),
        compiler_params=GRANT,
    )(shares, basis, local)


def neighbours(tail, head, axis):
    ends = lax.axis_size(axis) - 1
    return (
        lax.ppermute(tail, axis, [(i, i + 1) for i in range(ends)]),
        lax.ppermute(head, axis, [(i + 1, i) for i in range(ends)]),
    )


def body(residual, basis, inv_blocks, pattern, coarse_map, coarse_inv):
    nz = lax.axis_size("z")
    plane = lax.axis_size("h") * lax.axis_size("py")
    ncl, own_x, own_y = basis.shape
    vectors = residual.shape[2]
    slots = plane * ncl
    depth = nz * ncl

    columns = order_columns(coarse_inv, coarse_map.transpose(1, 2, 0))
    columns = columns.reshape(plane, ncl, 2 * depth)
    held = lax.all_to_all(columns, ("h", "py"), 0, 0).reshape(slots, 2 * depth)

    wanted = coarse_map.reshape(nz, slots)
    place = jnp.where(wanted // slots == lax.axis_index("z"), wanted % slots, -1)
    contrib = jnp.einsum("lxy,xyr->lr", basis, residual, precision=HIGH)
    sent = route(held, place, contrib)

    rounded = round_cells(residual, sent)
    below, above = neighbours(rounded[:, own_y - W :], rounded[:, :W], "py")
    first, last = widen(below, rounded, above)
    left, right = neighbours(last, first, ("z", "h"))
    partial = apply_block(lax.all_to_all(sent, "z", 0, 0))
    shares = lax.all_to_all(partial.reshape(plane, ncl, vectors), ("h", "py"), 0, 0)
    local_part = solve(pattern.reshape(-1), left, first, last, right, inv_blocks, partial, own_y)
    high = basis.astype(BF)
    low = (basis - high.astype(F32)).astype(BF)
    terms = jnp.concatenate([high, high, low], axis=0).transpose(1, 2, 0)
    terms = jnp.pad(terms, ((0, 0), (0, 0), (0, vectors - 3 * ncl)))
    return finish(shares, terms, local_part)


def solution(mesh):
    count_x, count_y = mesh.devices.shape
    fine = Mesh(mesh.devices.reshape(count_x // 2, 2, count_y), ("z", "h", "py"))
    px = ("z", "h")
    return jax.shard_map(
        body,
        mesh=fine,
        in_specs=(
            P(px, "py", None),
            P(None, px, "py"),
            P(px, "py", None, None, None, None),
            P(px, "py", None, None),
            P(),
            P(("z", "h", "py"), None),
        ),
        out_specs=P(px, "py", None),
        check_vma=False,
    )
```

```python
import functools

import jax
import jax.numpy as jnp
from jax import lax
from jax.experimental import pallas as pl
from jax.experimental.pallas import tpu as pltpu
from jax.sharding import Mesh, PartitionSpec as P

W = 8
K = 3
NCL = 4
BF = jnp.bfloat16
F32 = jnp.float32
HIGH = lax.Precision.HIGHEST
VMEM = pl.BlockSpec(memory_space=pltpu.VMEM)
HBM = pl.BlockSpec(memory_space=pltpu.HBM)
ANYWHERE = pl.BlockSpec(memory_space=pl.ANY)
LARGE = pltpu.CompilerParams(vmem_limit_bytes=60 * 1024 * 1024)
SLOW = pl.CostEstimate(flops=20_000_000_000, bytes_accessed=1_000_000, transcendentals=0)
SOLVE = pltpu.CompilerParams(vmem_limit_bytes=50 * 1024 * 1024)
GRANT = pltpu.CompilerParams(vmem_limit_bytes=32 * 1024 * 1024)


def order_kernel(rows_hbm, map_hbm, out_ref, rows_ref, map_ref, sems):
    fetch_map = pltpu.make_async_copy(map_hbm, map_ref, sems.at[0])
    fetch_rows = pltpu.make_async_copy(rows_hbm, rows_ref, sems.at[1])
    fetch_map.start()
    fetch_rows.start()
    ncl, total = rows_ref.shape
    ny, _, nx = map_ref.shape
    lanes = ncl * nx
    half = lanes // 2
    chunks = total // lanes
    to = lax.broadcasted_iota(jnp.int32, (lanes, lanes), 1)
    h, zm = to // half, to % half
    source = (zm % ncl) * nx + (zm // ncl) * 2 + h
    swap = (lax.broadcasted_iota(jnp.int32, (lanes, lanes), 0) == source).astype(F32).astype(BF)
    fetch_map.wait()
    flat = jnp.concatenate([map_ref[:, m, :] for m in range(ncl)], axis=1)
    upper_bits = (flat // 16).astype(F32).astype(BF)
    lower_bits = (flat % 16).astype(F32).astype(BF)
    ids = jnp.dot(upper_bits, swap, preferred_element_type=F32) * 16.0
    ids = (ids + jnp.dot(lower_bits, swap, preferred_element_type=F32)).astype(jnp.int32)
    fetch_rows.wait()
    upper = lax.broadcasted_iota(jnp.int32, (2 * ncl, lanes), 0) < ncl
    twice = [
        jnp.concatenate([rows_ref[:, s * lanes : (s + 1) * lanes]] * 2, axis=0) for s in range(chunks)
    ]
    done = []
    for pair in range(ny // 2):
        one, two = (jnp.broadcast_to(ids[2 * pair + i : 2 * pair + i + 1, :], upper.shape) for i in (0, 1))
        spot = jnp.where(upper, one, two)
        lane = spot % lanes
        chunk = spot // lanes
        picked = jnp.zeros(upper.shape, F32)
        for s in range(chunks):
            moved = jnp.take_along_axis(twice[s], lane, axis=1, mode="promise_in_bounds")
            picked = jnp.where(chunk == s, moved, picked)
        done.append(picked)
    picked = jnp.concatenate(done, axis=0)
    both = jnp.concatenate([picked, pltpu.roll(picked, half, 1)], axis=0)
    out_ref[...] = both.astype(BF)


def order_columns(rows, by_y):
    ny, ncl, nx = by_y.shape
    return pl.pallas_call(
        order_kernel,
        out_shape=jax.ShapeDtypeStruct((2 * ny * ncl, nx * ncl), BF),
        in_specs=[ANYWHERE, ANYWHERE],
        out_specs=VMEM,
        scratch_shapes=[
            pltpu.VMEM(rows.shape, F32),
            pltpu.VMEM(by_y.shape, jnp.int32),
            pltpu.SemaphoreType.DMA((2,)),
        ],
        compiler_params=LARGE,
    )(rows, by_y)


def route_kernel(held_ref, place_ref, contrib_ref, out_ref):
    held = held_ref.shape[0]
    slots = place_ref.shape[1]
    ncl = contrib_ref.shape[0]
    depth = out_ref.shape[1] - 2 * ncl
    turned = held_ref[...].astype(F32).T[:depth].astype(BF)
    rows = lax.broadcasted_iota(jnp.int32, (held, slots), 0)
    contrib = contrib_ref[...]
    coarse = contrib.astype(BF).astype(F32)
    both = jnp.concatenate([coarse, contrib - coarse], axis=0).astype(BF)
    for z in range(place_ref.shape[0]):
        pick = (rows == place_ref[z : z + 1, :]).astype(F32).astype(BF)
        sent = jnp.dot(turned, pick, preferred_element_type=F32)
        out_ref[z, 0:depth, :] = sent.astype(BF)
        out_ref[z, depth : depth + 2 * ncl, :] = both


def route(held, place, contrib):
    nz, slots = place.shape
    return pl.pallas_call(
        route_kernel,
        out_shape=jax.ShapeDtypeStruct((nz, (nz + 2) * contrib.shape[0], slots), BF),
        in_specs=[VMEM, VMEM, VMEM],
        out_specs=VMEM,
        compiler_params=GRANT,
        cost_estimate=SLOW,
    )(held, place, contrib)


def apply_kernel(got_ref, out_ref):
    nz, rows, lanes = got_ref.shape
    ncl = NCL
    depth = rows - 2 * ncl
    block = got_ref[0, 0:depth, :].astype(F32)
    for z in range(1, nz):
        block += got_ref[z, 0:depth, :].astype(F32)
    upper = lax.broadcasted_iota(jnp.int32, (2 * ncl, lanes), 0) < ncl
    high, low = [], []
    for q in range(nz // 2):
        one = got_ref[2 * q, depth:rows, :].astype(F32)
        two = got_ref[2 * q + 1, depth:rows, :].astype(F32)
        high.append(jnp.where(upper, one, pltpu.roll(two, ncl, 0)))
        low.append(jnp.where(upper, pltpu.roll(one, ncl, 0), two))
    turned = block.T.astype(BF)
    cells = jnp.concatenate(high + low, axis=0).astype(BF)
    out_ref[...] = jnp.dot(
        jnp.concatenate([turned, turned], axis=1), cells, preferred_element_type=F32
    )


def apply_block(got):
    slots = got.shape[2]
    return pl.pallas_call(
        apply_kernel,
        out_shape=jax.ShapeDtypeStruct((slots, slots), F32),
        in_specs=[VMEM],
        out_specs=VMEM,
        compiler_params=GRANT,
        cost_estimate=SLOW,
    )(got)


def round_kernel(cells_ref, after_ref, out_ref):
    out_ref[...] = cells_ref[...].astype(BF)


def round_cells(cells, after):
    block = pl.BlockSpec((cells.shape[0] // 4,) + cells.shape[1:], lambda i: (i, 0, 0))
    return pl.pallas_call(
        round_kernel,
        grid=(4,),
        out_shape=jax.ShapeDtypeStruct(cells.shape, BF),
        in_specs=[block, ANYWHERE],
        out_specs=block,
        compiler_params=GRANT,
    )(cells, after)


def widen_kernel(below_ref, mid_ref, above_ref, first_ref, last_ref):
    rows = first_ref.shape[0]
    for start, out_ref in ((0, first_ref), (rows, last_ref)):
        part = slice(start, start + rows)
        out_ref[...] = jnp.concatenate([below_ref[part], mid_ref[part], above_ref[part]], axis=1)


def widen(below, mid, above):
    wide = below.shape[1] + mid.shape[1] + above.shape[1]
    shape = jax.ShapeDtypeStruct((mid.shape[0] // 2, wide, mid.shape[2]), BF)
    return pl.pallas_call(
        widen_kernel,
        out_shape=(shape, shape),
        in_specs=[VMEM, VMEM, VMEM],
        out_specs=(VMEM, VMEM),
        compiler_params=GRANT,
    )(below, mid, above)


def solve_kernel(pattern_ref, left_ref, first_ref, last_ref, right_ref, inv_hbm, after_ref, out_ref, ext_ref, inv_ref, sems):
    own_x, own_y = out_ref.shape[:2]
    rows = left_ref.shape[0]
    parts = sems.shape[0]
    each = own_x // parts
    fetches = [
        pltpu.make_async_copy(
            inv_hbm.at[0, 0, pl.ds(W + part * each, each)], inv_ref.at[pl.ds(part * each, each)], sems.at[part]
        )
        for part in range(parts)
    ]
    for fetch in fetches:
        fetch.start()
    for i, ref in enumerate((left_ref, first_ref, last_ref, right_ref)):
        ext_ref[i * rows : (i + 1) * rows] = ref[...]
    for part in range(parts):
        fetches[part].wait()
        for i in range(part * each, (part + 1) * each):
            spot = (W + i) * K
            blocks = jnp.concatenate([inv_ref[i, k] for k in range(K)], axis=1)
            cells = jnp.concatenate([ext_ref[pattern_ref[spot + k]] for k in range(K)], axis=0)
            solved = jnp.dot(blocks, cells, preferred_element_type=F32)
            out_ref[i] = solved[W : W + own_y]


def solve(pattern, left, first, last, right, inv_blocks, after, own_y):
    parts = 4
    own_x = 2 * first.shape[0]
    wide, vectors = first.shape[1:]
    return pl.pallas_call(
        solve_kernel,
        in_specs=[pl.BlockSpec(memory_space=pltpu.SMEM), VMEM, VMEM, VMEM, VMEM, HBM, ANYWHERE],
        out_specs=VMEM,
        scratch_shapes=[
            pltpu.VMEM((2 * own_x, wide, vectors), BF),
            pltpu.VMEM((own_x, K, wide, wide), BF),
            pltpu.SemaphoreType.DMA((parts,)),
        ],
        out_shape=jax.ShapeDtypeStruct((own_x, own_y, vectors), F32),
        compiler_params=SOLVE,
    )(pattern, left, first, last, right, inv_blocks, after)


def finish_kernel(shares_ref, basis_ref, local_ref, out_hbm, out_ref, sems):
    ncl = NCL
    tile, lanes = 2 * ncl, shares_ref.shape[1]
    tiles = [shares_ref[i * tile : (i + 1) * tile, :] for i in range(shares_ref.shape[0] // tile)]
    while len(tiles) > 1:
        tiles = [tiles[i] + tiles[i + 1] for i in range(0, len(tiles), 2)]
    sol = tiles[0] + pltpu.roll(tiles[0], ncl, 0)
    high = sol.astype(BF).astype(F32)
    upper = lax.broadcasted_iota(jnp.int32, (tile, lanes), 0) < ncl
    terms = [jnp.where(upper, high, sol - high), jnp.where(upper, high, 0.0)]
    terms = jnp.concatenate(terms + [jnp.zeros((lanes - 2 * tile, lanes), F32)], axis=0).astype(BF)
    parts = sems.shape[0]
    each = out_ref.shape[0] // parts
    stores = []
    for part in range(parts):
        for x in range(part * each, (part + 1) * each):
            out_ref[x] = local_ref[x] + jnp.dot(basis_ref[x], terms, preferred_element_type=F32)
        rows = pl.ds(part * each, each)
        store = pltpu.make_async_copy(out_ref.at[rows], out_hbm.at[rows], sems.at[part])
        store.start()
        stores.append(store)
    for store in stores:
        store.wait()


def finish(shares, basis, local):
    return pl.pallas_call(
        finish_kernel,
        out_shape=jax.ShapeDtypeStruct(local.shape, F32),
        in_specs=[VMEM, VMEM, VMEM],
        out_specs=HBM,
        scratch_shapes=[pltpu.VMEM(local.shape, F32), pltpu.SemaphoreType.DMA((8,))],
        compiler_params=GRANT,
    )(shares, basis, local)


def neighbours(tail, head, axis):
    ends = lax.axis_size(axis) - 1
    return (
        lax.ppermute(tail, axis, [(i, i + 1) for i in range(ends)]),
        lax.ppermute(head, axis, [(i + 1, i) for i in range(ends)]),
    )


def body(residual, basis, inv_blocks, pattern, coarse_map, coarse_inv):
    nz = lax.axis_size("z")
    plane = lax.axis_size("h") * lax.axis_size("py")
    ncl, own_x, own_y = basis.shape
    vectors = residual.shape[2]
    slots = plane * ncl
    depth = nz * ncl

    columns = order_columns(coarse_inv, coarse_map.transpose(1, 2, 0))
    columns = columns.reshape(plane, ncl, 2 * depth)
    held = lax.all_to_all(columns, ("h", "py"), 0, 0).reshape(slots, 2 * depth)

    wanted = coarse_map.reshape(nz, slots)
    place = jnp.where(wanted // slots == lax.axis_index("z"), wanted % slots, -1)
    contrib = jnp.einsum("lxy,xyr->lr", basis, residual, precision=HIGH)
    sent = route(held, place, contrib)

    rounded = round_cells(residual, sent)
    below, above = neighbours(rounded[:, own_y - W :], rounded[:, :W], "py")
    first, last = widen(below, rounded, above)
    left, right = neighbours(last, first, ("z", "h"))
    partial = apply_block(lax.all_to_all(sent, "z", 0, 0))
    shares = lax.all_to_all(partial.reshape(plane, ncl, vectors), ("h", "py"), 0, 0)
    local_part = solve(pattern.reshape(-1), left, first, last, right, inv_blocks, partial, own_y)
    high = lax.reduce_precision(basis, 8, 7)
    terms = jnp.concatenate([high, high, basis - high], axis=0).astype(BF).transpose(1, 2, 0)
    terms = jnp.pad(terms, ((0, 0), (0, 0), (0, vectors - 3 * ncl)))
    return finish(shares.reshape(slots, vectors), terms, local_part)


def solution(mesh):
    count_x, count_y = mesh.devices.shape
    fine = Mesh(mesh.devices.reshape(count_x // 2, 2, count_y), ("z", "h", "py"))
    px = ("z", "h")
    return jax.shard_map(
        body,
        mesh=fine,
        in_specs=(
            P(px, "py", None),
            P(None, px, "py"),
            P(px, "py", None, None, None, None),
            P(px, "py", None, None),
            P(),
            P(("z", "h", "py"), None),
        ),
        out_specs=P(px, "py", None),
        check_vma=False,
    )
```

```python
import functools

import jax
import jax.numpy as jnp
from jax import lax
from jax.experimental import pallas as pl
from jax.experimental.pallas import tpu as pltpu
from jax.sharding import Mesh, PartitionSpec as P

W = 8
K = 3
NCL = 4
BF = jnp.bfloat16
F32 = jnp.float32
HIGH = lax.Precision.HIGHEST
VMEM = pl.BlockSpec(memory_space=pltpu.VMEM)
HBM = pl.BlockSpec(memory_space=pltpu.HBM)
ANYWHERE = pl.BlockSpec(memory_space=pl.ANY)
LARGE = pltpu.CompilerParams(vmem_limit_bytes=60 * 1024 * 1024)
SLOW = pl.CostEstimate(flops=20_000_000_000, bytes_accessed=1_000_000, transcendentals=0)
SOLVE = pltpu.CompilerParams(vmem_limit_bytes=50 * 1024 * 1024)
GRANT = pltpu.CompilerParams(vmem_limit_bytes=32 * 1024 * 1024)


def order_kernel(rows_hbm, map_hbm, out_ref, rows_ref, map_ref, sems):
    fetch_map = pltpu.make_async_copy(map_hbm, map_ref, sems.at[0])
    fetch_rows = pltpu.make_async_copy(rows_hbm, rows_ref, sems.at[1])
    fetch_map.start()
    fetch_rows.start()
    ncl, total = rows_ref.shape
    ny, _, nx = map_ref.shape
    lanes = ncl * nx
    half = lanes // 2
    chunks = total // lanes
    to = lax.broadcasted_iota(jnp.int32, (lanes, lanes), 1)
    h, zm = to // half, to % half
    source = (zm % ncl) * nx + (zm // ncl) * 2 + h
    swap = (lax.broadcasted_iota(jnp.int32, (lanes, lanes), 0) == source).astype(F32).astype(BF)
    fetch_map.wait()
    flat = jnp.concatenate([map_ref[:, m, :] for m in range(ncl)], axis=1)
    upper_bits = (flat // 16).astype(F32).astype(BF)
    lower_bits = (flat % 16).astype(F32).astype(BF)
    ids = jnp.dot(upper_bits, swap, preferred_element_type=F32) * 16.0
    ids = (ids + jnp.dot(lower_bits, swap, preferred_element_type=F32)).astype(jnp.int32)
    fetch_rows.wait()
    upper = lax.broadcasted_iota(jnp.int32, (2 * ncl, lanes), 0) < ncl
    twice = [
        jnp.concatenate([rows_ref[:, s * lanes : (s + 1) * lanes]] * 2, axis=0) for s in range(chunks)
    ]
    done = []
    for pair in range(ny // 2):
        one, two = (jnp.broadcast_to(ids[2 * pair + i : 2 * pair + i + 1, :], upper.shape) for i in (0, 1))
        spot = jnp.where(upper, one, two)
        lane = spot % lanes
        chunk = spot // lanes
        picked = jnp.zeros(upper.shape, F32)
        for s in range(chunks):
            moved = jnp.take_along_axis(twice[s], lane, axis=1, mode="promise_in_bounds")
            picked = jnp.where(chunk == s, moved, picked)
        done.append(picked)
    picked = jnp.concatenate(done, axis=0)
    both = jnp.concatenate([picked, pltpu.roll(picked, half, 1)], axis=0)
    out_ref[...] = both.astype(BF)


def order_columns(rows, by_y):
    ny, ncl, nx = by_y.shape
    return pl.pallas_call(
        order_kernel,
        out_shape=jax.ShapeDtypeStruct((2 * ny * ncl, nx * ncl), BF),
        in_specs=[ANYWHERE, ANYWHERE],
        out_specs=VMEM,
        scratch_shapes=[
            pltpu.VMEM(rows.shape, F32),
            pltpu.VMEM(by_y.shape, jnp.int32),
            pltpu.SemaphoreType.DMA((2,)),
        ],
        compiler_params=LARGE,
    )(rows, by_y)


def route_kernel(held_ref, place_ref, contrib_ref, out_ref):
    held = held_ref.shape[0]
    slots = place_ref.shape[1]
    ncl = contrib_ref.shape[0]
    tile = 4 * ncl
    depth = out_ref.shape[1] - tile
    turned = held_ref[...].astype(F32).T[:depth].astype(BF)
    rows = lax.broadcasted_iota(jnp.int32, (held, slots), 0)
    contrib = contrib_ref[...]
    coarse = contrib.astype(BF).astype(F32)
    both = jnp.concatenate([coarse, contrib - coarse, jnp.zeros((2 * ncl, slots), F32)], axis=0).astype(BF)
    for z in range(place_ref.shape[0]):
        pick = (rows == place_ref[z : z + 1, :]).astype(F32).astype(BF)
        sent = jnp.dot(turned, pick, preferred_element_type=F32)
        out_ref[z, 0:depth, :] = sent.astype(BF)
        out_ref[z, depth : depth + tile, :] = both


def route(held, place, contrib):
    nz, slots = place.shape
    return pl.pallas_call(
        route_kernel,
        out_shape=jax.ShapeDtypeStruct((nz, (nz + 4) * contrib.shape[0], slots), BF),
        in_specs=[VMEM, VMEM, VMEM],
        out_specs=VMEM,
        compiler_params=GRANT,
        cost_estimate=SLOW,
    )(held, place, contrib)


def apply_kernel(got_ref, out_ref):
    nz, rows, lanes = got_ref.shape
    ncl = NCL
    depth = rows - 4 * ncl
    block = got_ref[0, 0:depth, :].astype(F32)
    for z in range(1, nz):
        block += got_ref[z, 0:depth, :].astype(F32)
    upper = lax.broadcasted_iota(jnp.int32, (2 * ncl, lanes), 0) < ncl
    high, low = [], []
    for q in range(nz // 2):
        one = got_ref[2 * q, depth:rows, :].astype(F32)[: 2 * ncl]
        two = got_ref[2 * q + 1, depth:rows, :].astype(F32)[: 2 * ncl]
        high.append(jnp.where(upper, one, pltpu.roll(two, ncl, 0)))
        low.append(jnp.where(upper, pltpu.roll(one, ncl, 0), two))
    turned = block.T.astype(BF)
    cells = jnp.concatenate(high + low, axis=0).astype(BF)
    out_ref[...] = jnp.dot(
        jnp.concatenate([turned, turned], axis=1), cells, preferred_element_type=F32
    )


def apply_block(got):
    slots = got.shape[2]
    return pl.pallas_call(
        apply_kernel,
        out_shape=jax.ShapeDtypeStruct((slots, slots), F32),
        in_specs=[VMEM],
        out_specs=VMEM,
        compiler_params=GRANT,
        cost_estimate=SLOW,
    )(got)


def round_kernel(cells_ref, after_ref, out_ref):
    out_ref[...] = cells_ref[...].astype(BF)


def round_cells(cells, after):
    block = pl.BlockSpec((cells.shape[0] // 4,) + cells.shape[1:], lambda i: (i, 0, 0))
    return pl.pallas_call(
        round_kernel,
        grid=(4,),
        out_shape=jax.ShapeDtypeStruct(cells.shape, BF),
        in_specs=[block, ANYWHERE],
        out_specs=block,
        compiler_params=GRANT,
    )(cells, after)


def widen_kernel(below_ref, mid_ref, above_ref, first_ref, last_ref):
    rows = first_ref.shape[0]
    for start, out_ref in ((0, first_ref), (rows, last_ref)):
        part = slice(start, start + rows)
        below, above = below_ref[part][:, W:], above_ref[part][:, :W]
        out_ref[...] = jnp.concatenate([below, mid_ref[part], above], axis=1)


def widen(below, mid, above):
    wide = mid.shape[1] + 2 * W
    shape = jax.ShapeDtypeStruct((mid.shape[0] // 2, wide, mid.shape[2]), BF)
    return pl.pallas_call(
        widen_kernel,
        out_shape=(shape, shape),
        in_specs=[VMEM, VMEM, VMEM],
        out_specs=(VMEM, VMEM),
        compiler_params=GRANT,
    )(below, mid, above)


def solve_kernel(pattern_ref, left_ref, first_ref, last_ref, right_ref, inv_hbm, after_ref, out_ref, ext_ref, inv_ref, sems):
    own_x, own_y = out_ref.shape[:2]
    rows = left_ref.shape[0]
    parts = sems.shape[0]
    each = own_x // parts
    fetches = [
        pltpu.make_async_copy(
            inv_hbm.at[0, 0, pl.ds(W + part * each, each)], inv_ref.at[pl.ds(part * each, each)], sems.at[part]
        )
        for part in range(parts)
    ]
    for fetch in fetches:
        fetch.start()
    for i, ref in enumerate((left_ref, first_ref, last_ref, right_ref)):
        ext_ref[i * rows : (i + 1) * rows] = ref[...]
    for part in range(parts):
        fetches[part].wait()
        for i in range(part * each, (part + 1) * each):
            spot = (W + i) * K
            blocks = jnp.concatenate([inv_ref[i, k] for k in range(K)], axis=1)
            cells = jnp.concatenate([ext_ref[pattern_ref[spot + k]] for k in range(K)], axis=0)
            solved = jnp.dot(blocks, cells, preferred_element_type=F32)
            out_ref[i] = solved[W : W + own_y]


def solve(pattern, left, first, last, right, inv_blocks, after, own_y):
    parts = 4
    own_x = 2 * first.shape[0]
    wide, vectors = first.shape[1:]
    return pl.pallas_call(
        solve_kernel,
        in_specs=[pl.BlockSpec(memory_space=pltpu.SMEM), VMEM, VMEM, VMEM, VMEM, HBM, ANYWHERE],
        out_specs=VMEM,
        scratch_shapes=[
            pltpu.VMEM((2 * own_x, wide, vectors), BF),
            pltpu.VMEM((own_x, K, wide, wide), BF),
            pltpu.SemaphoreType.DMA((parts,)),
        ],
        out_shape=jax.ShapeDtypeStruct((own_x, own_y, vectors), F32),
        compiler_params=SOLVE,
    )(pattern, left, first, last, right, inv_blocks, after)


def finish_kernel(shares_ref, basis_ref, local_ref, out_hbm, out_ref, sems):
    ncl = NCL
    tile, lanes = 2 * ncl, shares_ref.shape[1]
    tiles = [shares_ref[i * tile : (i + 1) * tile, :] for i in range(shares_ref.shape[0] // tile)]
    while len(tiles) > 1:
        tiles = [tiles[i] + tiles[i + 1] for i in range(0, len(tiles), 2)]
    sol = tiles[0] + pltpu.roll(tiles[0], ncl, 0)
    high = sol.astype(BF).astype(F32)
    upper = lax.broadcasted_iota(jnp.int32, (tile, lanes), 0) < ncl
    terms = [jnp.where(upper, high, sol - high), jnp.where(upper, high, 0.0)]
    terms = jnp.concatenate(terms + [jnp.zeros((lanes - 2 * tile, lanes), F32)], axis=0).astype(BF)
    parts = sems.shape[0]
    each = out_ref.shape[0] // parts
    stores = []
    for part in range(parts):
        for x in range(part * each, (part + 1) * each):
            out_ref[x] = local_ref[x] + jnp.dot(basis_ref[x], terms, preferred_element_type=F32)
        rows = pl.ds(part * each, each)
        store = pltpu.make_async_copy(out_ref.at[rows], out_hbm.at[rows], sems.at[part])
        store.start()
        stores.append(store)
    for store in stores:
        store.wait()


def finish(shares, basis, local):
    return pl.pallas_call(
        finish_kernel,
        out_shape=jax.ShapeDtypeStruct(local.shape, F32),
        in_specs=[VMEM, VMEM, VMEM],
        out_specs=HBM,
        scratch_shapes=[pltpu.VMEM(local.shape, F32), pltpu.SemaphoreType.DMA((8,))],
        compiler_params=GRANT,
    )(shares, basis, local)


def neighbours(tail, head, axis):
    ends = lax.axis_size(axis) - 1
    return (
        lax.ppermute(tail, axis, [(i, i + 1) for i in range(ends)]),
        lax.ppermute(head, axis, [(i + 1, i) for i in range(ends)]),
    )


def body(residual, basis, inv_blocks, pattern, coarse_map, coarse_inv):
    nz = lax.axis_size("z")
    plane = lax.axis_size("h") * lax.axis_size("py")
    ncl, own_x, own_y = basis.shape
    vectors = residual.shape[2]
    slots = plane * ncl
    depth = nz * ncl

    columns = order_columns(coarse_inv, coarse_map.transpose(1, 2, 0))
    columns = columns.reshape(plane, ncl, 2 * depth)
    held = lax.all_to_all(columns, ("h", "py"), 0, 0).reshape(slots, 2 * depth)

    wanted = coarse_map.reshape(nz, slots)
    place = jnp.where(wanted // slots == lax.axis_index("z"), wanted % slots, -1)
    contrib = jnp.einsum("lxy,xyr->lr", basis, residual, precision=HIGH)
    sent = route(held, place, contrib)

    rounded = round_cells(residual, sent)
    below, above = neighbours(rounded[:, own_y - 2 * W :], rounded[:, : 2 * W], "py")
    first, last = widen(below, rounded, above)
    left, right = neighbours(last, first, ("z", "h"))
    partial = apply_block(lax.all_to_all(sent, "z", 0, 0))
    shares = lax.all_to_all(partial.reshape(plane, ncl, vectors), ("h", "py"), 0, 0)
    local_part = solve(pattern.reshape(-1), left, first, last, right, inv_blocks, partial, own_y)
    high = lax.reduce_precision(basis, 8, 7)
    terms = jnp.concatenate([high, high, basis - high], axis=0).astype(BF).transpose(1, 2, 0)
    terms = jnp.pad(terms, ((0, 0), (0, 0), (0, vectors - 3 * ncl)))
    return finish(shares.reshape(slots, vectors), terms, local_part)


def solution(mesh):
    count_x, count_y = mesh.devices.shape
    fine = Mesh(mesh.devices.reshape(count_x // 2, 2, count_y), ("z", "h", "py"))
    px = ("z", "h")
    return jax.shard_map(
        body,
        mesh=fine,
        in_specs=(
            P(px, "py", None),
            P(None, px, "py"),
            P(px, "py", None, None, None, None),
            P(px, "py", None, None),
            P(),
            P(("z", "h", "py"), None),
        ),
        out_specs=P(px, "py", None),
        check_vma=False,
    )
```

```python
import functools

import jax
import jax.numpy as jnp
from jax import lax
from jax.experimental import pallas as pl
from jax.experimental.pallas import tpu as pltpu
from jax.sharding import Mesh, PartitionSpec as P

W = 8
K = 3
NCL = 4
BF = jnp.bfloat16
F32 = jnp.float32
HIGH = lax.Precision.HIGHEST
VMEM = pl.BlockSpec(memory_space=pltpu.VMEM)
HBM = pl.BlockSpec(memory_space=pltpu.HBM)
ANYWHERE = pl.BlockSpec(memory_space=pl.ANY)
LARGE = pltpu.CompilerParams(vmem_limit_bytes=60 * 1024 * 1024)
SLOW = pl.CostEstimate(flops=20_000_000_000, bytes_accessed=1_000_000, transcendentals=0)
SOLVE = pltpu.CompilerParams(vmem_limit_bytes=50 * 1024 * 1024)
GRANT = pltpu.CompilerParams(vmem_limit_bytes=32 * 1024 * 1024)


def order_kernel(rows_hbm, map_hbm, out_ref, rows_ref, map_ref, sems):
    fetch_map = pltpu.make_async_copy(map_hbm, map_ref, sems.at[0])
    fetch_rows = pltpu.make_async_copy(rows_hbm, rows_ref, sems.at[1])
    fetch_map.start()
    fetch_rows.start()
    ncl, total = rows_ref.shape
    ny, _, nx = map_ref.shape
    lanes = ncl * nx
    half = lanes // 2
    chunks = total // lanes
    to = lax.broadcasted_iota(jnp.int32, (lanes, lanes), 1)
    h, zm = to // half, to % half
    source = (zm % ncl) * nx + (zm // ncl) * 2 + h
    swap = (lax.broadcasted_iota(jnp.int32, (lanes, lanes), 0) == source).astype(F32).astype(BF)
    fetch_map.wait()
    flat = jnp.concatenate([map_ref[:, m, :] for m in range(ncl)], axis=1)
    upper_bits = (flat // 16).astype(F32).astype(BF)
    lower_bits = (flat % 16).astype(F32).astype(BF)
    ids = jnp.dot(upper_bits, swap, preferred_element_type=F32) * 16.0
    ids = (ids + jnp.dot(lower_bits, swap, preferred_element_type=F32)).astype(jnp.int32)
    fetch_rows.wait()
    upper = lax.broadcasted_iota(jnp.int32, (2 * ncl, lanes), 0) < ncl
    twice = [
        jnp.concatenate([rows_ref[:, s * lanes : (s + 1) * lanes]] * 2, axis=0) for s in range(chunks)
    ]
    done = []
    for pair in range(ny // 2):
        one, two = (jnp.broadcast_to(ids[2 * pair + i : 2 * pair + i + 1, :], upper.shape) for i in (0, 1))
        spot = jnp.where(upper, one, two)
        lane = spot % lanes
        chunk = spot // lanes
        picked = jnp.zeros(upper.shape, F32)
        for s in range(chunks):
            moved = jnp.take_along_axis(twice[s], lane, axis=1, mode="promise_in_bounds")
            picked = jnp.where(chunk == s, moved, picked)
        done.append(picked)
    picked = jnp.concatenate(done, axis=0)
    both = jnp.concatenate([picked, pltpu.roll(picked, half, 1)], axis=0)
    out_ref[...] = both.astype(BF)


def order_columns(rows, by_y):
    ny, ncl, nx = by_y.shape
    return pl.pallas_call(
        order_kernel,
        out_shape=jax.ShapeDtypeStruct((2 * ny * ncl, nx * ncl), BF),
        in_specs=[ANYWHERE, ANYWHERE],
        out_specs=VMEM,
        scratch_shapes=[
            pltpu.VMEM(rows.shape, F32),
            pltpu.VMEM(by_y.shape, jnp.int32),
            pltpu.SemaphoreType.DMA((2,)),
        ],
        compiler_params=LARGE,
    )(rows, by_y)


def route_kernel(held_ref, place_ref, contrib_ref, out_ref):
    held = held_ref.shape[0]
    slots = place_ref.shape[1]
    ncl = contrib_ref.shape[0]
    depth = out_ref.shape[1] - 2 * ncl
    turned = held_ref[...].astype(F32).T[:depth].astype(BF)
    rows = lax.broadcasted_iota(jnp.int32, (held, slots), 0)
    contrib = contrib_ref[...]
    coarse = contrib.astype(BF).astype(F32)
    both = jnp.concatenate([coarse, contrib - coarse], axis=0).astype(BF)
    for z in range(place_ref.shape[0]):
        pick = (rows == place_ref[z : z + 1, :]).astype(F32).astype(BF)
        sent = jnp.dot(turned, pick, preferred_element_type=F32)
        out_ref[z, 0:depth, :] = sent.astype(BF)
        out_ref[z, depth : depth + 2 * ncl, :] = both


def route(held, place, contrib):
    nz, slots = place.shape
    return pl.pallas_call(
        route_kernel,
        out_shape=jax.ShapeDtypeStruct((nz, (nz + 2) * contrib.shape[0], slots), BF),
        in_specs=[VMEM, VMEM, VMEM],
        out_specs=VMEM,
        compiler_params=GRANT,
        cost_estimate=SLOW,
    )(held, place, contrib)


def apply_kernel(got_ref, out_ref):
    nz, rows, lanes = got_ref.shape
    ncl = NCL
    depth = rows - 2 * ncl
    block = got_ref[0, 0:depth, :].astype(F32)
    for z in range(1, nz):
        block += got_ref[z, 0:depth, :].astype(F32)
    upper = lax.broadcasted_iota(jnp.int32, (2 * ncl, lanes), 0) < ncl
    high, low = [], []
    for q in range(nz // 2):
        one = got_ref[2 * q, depth:rows, :].astype(F32)
        two = got_ref[2 * q + 1, depth:rows, :].astype(F32)
        high.append(jnp.where(upper, one, pltpu.roll(two, ncl, 0)))
        low.append(jnp.where(upper, pltpu.roll(one, ncl, 0), two))
    turned = block.T.astype(BF)
    cells = jnp.concatenate(high + low, axis=0).astype(BF)
    out_ref[...] = jnp.dot(
        jnp.concatenate([turned, turned], axis=1), cells, preferred_element_type=F32
    )


def apply_block(got):
    slots = got.shape[2]
    return pl.pallas_call(
        apply_kernel,
        out_shape=jax.ShapeDtypeStruct((slots, slots), F32),
        in_specs=[VMEM],
        out_specs=VMEM,
        compiler_params=GRANT,
        cost_estimate=SLOW,
    )(got)


def round_kernel(cells_ref, after_ref, out_ref):
    out_ref[...] = cells_ref[...].astype(BF)


def round_cells(cells, after):
    block = pl.BlockSpec((cells.shape[0] // 4,) + cells.shape[1:], lambda i: (i, 0, 0))
    return pl.pallas_call(
        round_kernel,
        grid=(4,),
        out_shape=jax.ShapeDtypeStruct(cells.shape, BF),
        in_specs=[block, ANYWHERE],
        out_specs=block,
        compiler_params=GRANT,
    )(cells, after)


def widen_kernel(below_ref, mid_ref, above_ref, first_ref, last_ref):
    rows = first_ref.shape[0]
    for start, out_ref in ((0, first_ref), (rows, last_ref)):
        part = slice(start, start + rows)
        out_ref[...] = jnp.concatenate([below_ref[part], mid_ref[part], above_ref[part]], axis=1)


def widen(below, mid, above):
    wide = below.shape[1] + mid.shape[1] + above.shape[1]
    shape = jax.ShapeDtypeStruct((mid.shape[0] // 2, wide, mid.shape[2]), BF)
    return pl.pallas_call(
        widen_kernel,
        out_shape=(shape, shape),
        in_specs=[VMEM, VMEM, VMEM],
        out_specs=(VMEM, VMEM),
        compiler_params=GRANT,
    )(below, mid, above)


def solve_kernel(pattern_ref, left_ref, first_ref, last_ref, right_ref, inv_hbm, after_ref, out_ref, ext_ref, inv_ref, sems):
    own_x, own_y = out_ref.shape[:2]
    rows = left_ref.shape[0]
    parts = sems.shape[0]
    each = own_x // parts
    fetches = [
        pltpu.make_async_copy(
            inv_hbm.at[0, 0, pl.ds(W + part * each, each)], inv_ref.at[pl.ds(part * each, each)], sems.at[part]
        )
        for part in range(parts)
    ]
    for fetch in fetches:
        fetch.start()
    for i, ref in enumerate((left_ref, first_ref, last_ref, right_ref)):
        ext_ref[i * rows : (i + 1) * rows] = ref[...]
    for part in range(parts):
        fetches[part].wait()
        for i in range(part * each, (part + 1) * each):
            spot = (W + i) * K
            blocks = jnp.concatenate([inv_ref[i, k] for k in range(K)], axis=1)
            cells = jnp.concatenate([ext_ref[pattern_ref[spot + k]] for k in range(K)], axis=0)
            solved = jnp.dot(blocks, cells, preferred_element_type=F32)
            out_ref[i] = solved[W : W + own_y]


def solve(pattern, left, first, last, right, inv_blocks, after, own_y):
    parts = 4
    own_x = 2 * first.shape[0]
    wide, vectors = first.shape[1:]
    return pl.pallas_call(
        solve_kernel,
        in_specs=[pl.BlockSpec(memory_space=pltpu.SMEM), VMEM, VMEM, VMEM, VMEM, HBM, ANYWHERE],
        out_specs=VMEM,
        scratch_shapes=[
            pltpu.VMEM((2 * own_x, wide, vectors), BF),
            pltpu.VMEM((own_x, K, wide, wide), BF),
            pltpu.SemaphoreType.DMA((parts,)),
        ],
        out_shape=jax.ShapeDtypeStruct((own_x, own_y, vectors), F32),
        compiler_params=SOLVE,
    )(pattern, left, first, last, right, inv_blocks, after)


def finish_kernel(shares_ref, basis_ref, local_ref, out_hbm, out_ref, sems):
    ncl = NCL
    tile, lanes = 2 * ncl, shares_ref.shape[1]
    tiles = [shares_ref[i * tile : (i + 1) * tile, :] for i in range(shares_ref.shape[0] // tile)]
    while len(tiles) > 1:
        tiles = [tiles[i] + tiles[i + 1] for i in range(0, len(tiles), 2)]
    sol = tiles[0] + pltpu.roll(tiles[0], ncl, 0)
    high = sol.astype(BF).astype(F32)
    upper = lax.broadcasted_iota(jnp.int32, (tile, lanes), 0) < ncl
    terms = [jnp.where(upper, high, sol - high), jnp.where(upper, high, 0.0)]
    terms = jnp.concatenate(terms + [jnp.zeros((lanes - 2 * tile, lanes), F32)], axis=0).astype(BF)
    parts = sems.shape[0]
    each = out_ref.shape[0] // parts
    stores = []
    for part in range(parts):
        for x in range(part * each, (part + 1) * each):
            out_ref[x] = local_ref[x] + jnp.dot(basis_ref[x], terms, preferred_element_type=F32)
        rows = pl.ds(part * each, each)
        store = pltpu.make_async_copy(out_ref.at[rows], out_hbm.at[rows], sems.at[part])
        store.start()
        stores.append(store)
    for store in stores:
        store.wait()


def finish(shares, basis, local):
    return pl.pallas_call(
        finish_kernel,
        out_shape=jax.ShapeDtypeStruct(local.shape, F32),
        in_specs=[VMEM, VMEM, VMEM],
        out_specs=HBM,
        scratch_shapes=[pltpu.VMEM(local.shape, F32), pltpu.SemaphoreType.DMA((8,))],
        compiler_params=GRANT,
    )(shares, basis, local)


def neighbours(tail, head, axis):
    count = lax.axis_size(axis)
    odd = lax.axis_index(axis) % 2 == 1
    one = lax.ppermute(jnp.where(odd, head, tail), axis, [(i, i ^ 1) for i in range(count)])
    inner = range(1, count - 1)
    two = lax.ppermute(jnp.where(odd, tail, head), axis, [(i, ((i + 1) ^ 1) - 1) for i in inner])
    return jnp.where(odd, one, two), jnp.where(odd, two, one)


def body(residual, basis, inv_blocks, pattern, coarse_map, coarse_inv):
    nz = lax.axis_size("z")
    plane = lax.axis_size("h") * lax.axis_size("py")
    ncl, own_x, own_y = basis.shape
    vectors = residual.shape[2]
    slots = plane * ncl
    depth = nz * ncl

    columns = order_columns(coarse_inv, coarse_map.transpose(1, 2, 0))
    columns = columns.reshape(plane, ncl, 2 * depth)
    held = lax.all_to_all(columns, ("h", "py"), 0, 0).reshape(slots, 2 * depth)

    wanted = coarse_map.reshape(nz, slots)
    place = jnp.where(wanted // slots == lax.axis_index("z"), wanted % slots, -1)
    contrib = jnp.einsum("lxy,xyr->lr", basis, residual, precision=HIGH)
    sent = route(held, place, contrib)

    rounded = round_cells(residual, sent)
    below, above = neighbours(rounded[:, own_y - W :], rounded[:, :W], "py")
    first, last = widen(below, rounded, above)
    left, right = neighbours(last, first, ("z", "h"))
    partial = apply_block(lax.all_to_all(sent, "z", 0, 0))
    shares = lax.all_to_all(partial.reshape(plane, ncl, vectors), ("h", "py"), 0, 0)
    local_part = solve(pattern.reshape(-1), left, first, last, right, inv_blocks, partial, own_y)
    high = lax.reduce_precision(basis, 8, 7)
    terms = jnp.concatenate([high, high, basis - high], axis=0).astype(BF).transpose(1, 2, 0)
    terms = jnp.pad(terms, ((0, 0), (0, 0), (0, vectors - 3 * ncl)))
    return finish(shares.reshape(slots, vectors), terms, local_part)


def solution(mesh):
    count_x, count_y = mesh.devices.shape
    fine = Mesh(mesh.devices.reshape(count_x // 2, 2, count_y), ("z", "h", "py"))
    px = ("z", "h")
    return jax.shard_map(
        body,
        mesh=fine,
        in_specs=(
            P(px, "py", None),
            P(None, px, "py"),
            P(px, "py", None, None, None, None),
            P(px, "py", None, None),
            P(),
            P(("z", "h", "py"), None),
        ),
        out_specs=P(px, "py", None),
        check_vma=False,
    )
```
